32 devices in a mesh: node: 8 (over y, x, core), edge: 4 (over z).
Axes of the slice: x: 2, y: 2, z: 4, core: 2. Of those that a mesh axis runs over, the one named last changes fastest.
Arguments:
- embed: bfloat16 [8192, 256], P('node'), may hold values from -6 to 6
- cotangent: bfloat16 [8192, 256], P('node'), may hold values from -6 to 6
- values: bfloat16 [8, 4, 128, 128, 128], P('node', 'edge'), may hold values from 0.0023345947 to 0.0390625
- block_slot: int32 [8, 4, 128], P('node', 'edge'), may hold values from 0 to 7
- block_col: int32 [8, 4, 128], P('node', 'edge'), may hold values from 0 to 7
- block_count: int32 [8, 4], P('node', 'edge'), may hold values from 16 to 128, as said below
- slot_rows: int32 [8, 8], P('node'), may hold values from 0 to 7
Outputs:
- final: bfloat16 [8192, 256], P(('node', 'edge'))
- grad: bfloat16 [8192, 256], P(('node', 'edge'))
The draws below stay inside these ranges and needn't reach their ends.
Inputs may be any that keep to these rules, and one draw needn't show every extreme that they name: `block_count`: slots at and past a device's count are padding. Some device uses all 128 slots in every draw.
All inputs are finite; a program needn't handle non-finite values.
Results may differ from the reference program's by a relative error of at most 0.0026.
Values may be sent and summed in bfloat16 or wider, within the bound.
A program may use at most 128 MiB of HBM per device.

```python
import math
import jax
import jax.numpy as jnp
from jax import lax

D = 256
BS = 128
LAYERS = 2
GB = 8
EB = 128
NODES = 8192
N_NODE = 8
N_EDGE = 4


def draw_block_count(key, part):
    level = jax.random.randint(jax.random.fold_in(key, 11), (N_NODE * N_EDGE,), 0, 4)
    table = jnp.array([EB, EB // 2, EB // 4, EB // 8], dtype=jnp.int32)
    counts = table[level]
    fullest = jax.random.randint(jax.random.fold_in(key, 12), (), 0, N_NODE * N_EDGE)
    counts = counts.at[fullest].set(EB)
    return counts.reshape(N_NODE, N_EDGE).astype(jnp.int32)


def set_ends(result, key, least, top_value):
    spot = [jax.random.randint(jax.random.fold_in(key, axis), (), 0, length) for axis, length in enumerate(result.shape)]
    widest = result.shape.index(max(result.shape))
    next_to = spot[:widest] + [(spot[widest] + 1) % result.shape[widest]] + spot[widest + 1:]
    return result.at[tuple(spot)].set(least).at[tuple(next_to)].set(top_value)


def steps_of(stream_key, shape, split, smallest, top_value):
    loudness = 1.0
    for axis_at, blocks in split:
        heights = jax.random.uniform(jax.random.fold_in(jax.random.fold_in(stream_key, 6), axis_at), (blocks,), jnp.float32, smallest / len(split), top_value / len(split))
        loudness = loudness * jnp.repeat(jnp.exp(heights), shape[axis_at] // blocks).reshape((-1,) + (1,) * (len(shape) - 1 - axis_at))
    return loudness


def bell_draw(rng, shape, deviation, bound, split=(), kind=jnp.bfloat16):
    drawn = deviation * jax.random.normal(rng, shape, jnp.float32)
    if split:
        drawn = drawn * steps_of(rng, shape, split, -0.22, 0.18)
    return jnp.clip(drawn, -bound, bound).astype(kind)


def setup_inputs(seed: int = 0) -> dict:
    streams_of = jax.random.split(jax.random.key(seed), 8)
    embed = bell_draw(streams_of[0], (NODES, D), 1.0, 6.0, ((0, 8),))
    cotangent = bell_draw(streams_of[1], (NODES, D), 1.0, 6.0, ((0, 8),))
    values = jnp.clip(jnp.exp(math.log(0.0390625) - 2.8173246 * jax.random.uniform(streams_of[2], (N_NODE, N_EDGE, EB, BS, BS), jnp.float32) ** steps_of(streams_of[2], (N_NODE, N_EDGE, EB, BS, BS), ((0, 8), (1, 4)), -0.2, 0.2)), 0.0023345947, 0.0390625).astype(jnp.bfloat16)
    block_slot = set_ends(jax.random.randint(streams_of[3], (N_NODE, N_EDGE, EB), 0, N_NODE), jax.random.fold_in(streams_of[3], 1), 0, N_NODE - 1).astype(jnp.int32)
    block_col = set_ends(jax.random.randint(streams_of[4], (N_NODE, N_EDGE, EB), 0, GB), jax.random.fold_in(streams_of[4], 1), 0, GB - 1).astype(jnp.int32)
    block_count = draw_block_count(jax.random.fold_in(streams_of[7], 71), 0)
    slot_rows = set_ends(jax.random.randint(streams_of[6], (N_NODE, N_NODE), 0, GB), jax.random.fold_in(streams_of[6], 1), 0, GB - 1).astype(jnp.int32)
    return {"embed": embed, "cotangent": cotangent, "values": values, "block_slot": block_slot, "block_col": block_col, "block_count": block_count, "slot_rows": slot_rows}


def to_blocks(rows):
    return rows.reshape(N_NODE, BS, GB, D).transpose(0, 2, 1, 3)


def from_blocks(blocks):
    return blocks.transpose(0, 2, 1, 3).reshape(N_NODE * BS * GB, D)


def device_items(values, block_slot, block_col, block_count):
    owners = jnp.repeat(jnp.arange(N_NODE, dtype=jnp.int32), N_EDGE)
    return (owners, values.reshape(N_NODE * N_EDGE, EB, BS, BS),
            block_slot.reshape(N_NODE * N_EDGE, EB), block_col.reshape(N_NODE * N_EDGE, EB),
            block_count.reshape(N_NODE * N_EDGE))


def forward_layer(source, items, slot_rows):
    targets = jnp.arange(N_NODE, dtype=jnp.int32)

    def per_device(total, item):
        owner, vals, slots, cols, count = item
        live = (jnp.arange(EB, dtype=jnp.int32) < count).astype(jnp.float32)
        picked = source[owner][cols].astype(jnp.float32)
        prods = jnp.einsum("bij,bjd->bid", vals.astype(jnp.float32), picked) * live[:, None, None]
        parts = jnp.zeros((N_NODE, BS, D), jnp.float32).at[slots].add(prods)
        total = total.at[targets, slot_rows[:, owner]].add(parts)
        return total, None

    start = jnp.zeros((N_NODE, GB, BS, D), jnp.float32)
    total, _ = lax.scan(per_device, start, items)
    return total


def backward_layer(grads, items, slot_rows):
    targets = jnp.arange(N_NODE, dtype=jnp.int32)

    def per_device(total, item):
        owner, vals, slots, cols, count = item
        live = (jnp.arange(EB, dtype=jnp.int32) < count).astype(jnp.float32)
        wanted = grads[targets, slot_rows[:, owner]]
        picked = wanted[slots].astype(jnp.float32)
        prods = jnp.einsum("bij,bid->bjd", vals.astype(jnp.float32), picked) * live[:, None, None]
        local = jnp.zeros((GB, BS, D), jnp.float32).at[cols].add(prods)
        return total.at[owner].add(local), None

    start = jnp.zeros((N_NODE, GB, BS, D), jnp.float32)
    total, _ = lax.scan(per_device, start, items)
    return total


def propagate(start_rows, layer_fn, items, slot_rows):
    current = to_blocks(start_rows)
    total = current.astype(jnp.float32)
    for layer in range(LAYERS):
        nxt = layer_fn(current, items, slot_rows)
        if layer + 1 < LAYERS:
            current = lax.optimization_barrier(nxt.astype(jnp.bfloat16))
            total = total + current.astype(jnp.float32)
        else:
            total = total + nxt
    return from_blocks(total / float(LAYERS + 1)).astype(jnp.bfloat16)


def reference(embed, cotangent, values, block_slot, block_col, block_count, slot_rows):
    items = device_items(values, block_slot, block_col, block_count)
    final = propagate(embed, forward_layer, items, slot_rows)
    grad = propagate(cotangent, backward_layer, items, slot_rows)
    return final, grad
```

```python
import jax
import jax.numpy as jnp
from jax import lax
from jax.experimental import pallas as pl
from jax.experimental.pallas import tpu as pltpu
from jax.sharding import PartitionSpec as P

LAYERS = 2
CHUNK = 16


def dense_kernel(slots_ref, cols_ref, count_ref, vals_ref, out_ref, acc):
    turn = pl.program_id(0)
    groups, sources, size, _ = acc.shape
    width, _, part, _ = out_ref.shape

    @pl.when(turn == 0)
    def _():
        acc[...] = jnp.zeros_like(acc)

    begin = turn * CHUNK
    live = jnp.clip(count_ref[0] - begin, 0, CHUNK)

    def add(b, carry):
        s, c = slots_ref[begin + b], cols_ref[begin + b]
        acc[s, c] += vals_ref[b].astype(jnp.float32)
        return carry

    lax.fori_loop(0, live, add, 0)

    @pl.when(turn == pl.num_programs(0) - 1)
    def _():
        def put(s, carry):
            for c in range(sources):
                for e in range(width):
                    out_ref[e, s, :, c * size:(c + 1) * size] = acc[
                        s, c, e * part:(e + 1) * part, :
                    ].astype(out_ref.dtype)
            return carry

        lax.fori_loop(0, groups, put, 0)


def dense_adjacency(vals, slots, cols, count, groups, sources, width):
    total, size, _ = vals.shape
    part = size // width
    return pl.pallas_call(
        dense_kernel,
        out_shape=jax.ShapeDtypeStruct((width, groups, part, sources * size), jnp.bfloat16),
        grid_spec=pltpu.PrefetchScalarGridSpec(
            num_scalar_prefetch=3,
            grid=(total // CHUNK,),
            in_specs=[pl.BlockSpec((CHUNK, size, size), lambda t, *_: (t, 0, 0))],
            out_specs=pl.BlockSpec(
                (width, groups, part, sources * size), lambda t, *_: (0, 0, 0, 0)
            ),
            scratch_shapes=[pltpu.VMEM((groups, sources, size, size), jnp.float32)],
        ),
        compiler_params=pltpu.CompilerParams(
            dimension_semantics=("arbitrary",), vmem_limit_bytes=56 * 1024 * 1024
        ),
    )(slots, cols, count, vals)


def shards(embed, cotangent, values, block_slot, block_col, block_count, slot_rows):
    width = lax.axis_size("edge")
    place = lax.axis_index("edge")
    groups = slot_rows.shape[1]
    vals = values[0, 0]
    size = vals.shape[1]
    part = size // width
    sources = embed.shape[0] // size
    depth = embed.shape[1]
    slot_index = slot_rows[0]

    dense = dense_adjacency(
        vals, block_slot[0, 0], block_col[0, 0], block_count[0], groups, sources, width
    )
    dense = dense.reshape(width * groups * part, sources * size)

    def share_of(rows):
        rows = lax.dynamic_slice_in_dim(rows, place * (sources * part), sources * part, 0)
        return rows.reshape(part, sources, depth).transpose(1, 0, 2)

    def forward(source):
        return jnp.dot(
            dense, source.reshape(sources * size, depth), preferred_element_type=jnp.float32
        ).reshape(width, groups * part, depth)

    def backward(wanted):
        out = lax.dot_general(
            dense,
            wanted.reshape(width * groups * part, depth),
            (((0,), (0,)), ((), ())),
            preferred_element_type=jnp.float32,
        )
        out = out.reshape(sources, width, part, depth).transpose(1, 0, 2, 3)
        return out.reshape(width, sources * part, depth)

    def place_rows(arrived):
        hit = slot_index[None, :] == jnp.arange(sources, dtype=jnp.int32)[:, None]
        terms = jnp.where(hit[:, :, None, None], arrived.astype(jnp.float32)[None], 0.0)
        return terms.sum(1)

    def exchange(x):
        return lax.all_to_all(x, "node", split_axis=0, concat_axis=0, tiled=True)

    embed_share, cot_share = share_of(embed), share_of(cotangent)

    wanted = lax.all_gather(exchange(cot_share[slot_index]), "edge", axis=0)
    source = embed.reshape(size, sources, depth).transpose(1, 0, 2)

    sums = jnp.concatenate([forward(source), backward(wanted)], axis=1).astype(jnp.bfloat16)
    sums = lax.psum_scatter(sums, "edge", scatter_dimension=0, tiled=False)
    parts = sums[: groups * part].reshape(groups, part, depth)
    back = sums[groups * part:].reshape(sources, part, depth)
    arrived = exchange(jnp.stack([parts, back[slot_index]], axis=1))
    layer = place_rows(arrived[:, 0]).astype(jnp.bfloat16)
    gathered = lax.all_gather(
        jnp.concatenate([layer, arrived[:, 1]], axis=0), "edge", axis=0
    )
    source = gathered[:, :sources].transpose(1, 0, 2, 3)
    wanted = gathered[:, sources:]

    sums = jnp.concatenate([forward(source), backward(wanted)], axis=1)
    sums = lax.psum_scatter(sums, "edge", scatter_dimension=0, tiled=False)
    top = place_rows(exchange(sums[: groups * part].reshape(groups, part, depth)))
    top_back = sums[groups * part:].reshape(sources, part, depth)

    def mean(first, second, third):
        total = first.astype(jnp.float32) + second.astype(jnp.float32) + third
        total = (total / float(LAYERS + 1)).astype(jnp.bfloat16)
        return total.transpose(1, 0, 2).reshape(part * sources, depth)

    return mean(embed_share, layer, top), mean(cot_share, back, top_back)


def solution(mesh):
    placed = (
        P("node", None),
        P("node", None),
        P("node", "edge", None, None, None),
        P("node", "edge", None),
        P("node", "edge", None),
        P("node", "edge"),
        P("node", None),
    )
    return jax.shard_map(
        shards,
        mesh=mesh,
        in_specs=placed,
        out_specs=(P(("node", "edge"), None), P(("node", "edge"), None)),
        check_vma=False,
    )
```

```python
import jax
import jax.numpy as jnp
from jax import lax
from jax.experimental import pallas as pl
from jax.experimental.pallas import tpu as pltpu
from jax.sharding import PartitionSpec as P

LAYERS = 2
CHUNK = 16


def dense_kernel(slots_ref, cols_ref, count_ref, vals_ref, out_ref, acc):
    turn = pl.program_id(0)
    groups, sources, size, _ = acc.shape
    width, _, part, _ = out_ref.shape

    @pl.when(turn == 0)
    def _():
        acc[...] = jnp.zeros_like(acc)

    begin = turn * CHUNK
    live = jnp.clip(count_ref[0] - begin, 0, CHUNK)

    def add(b, carry):
        s, c = slots_ref[begin + b], cols_ref[begin + b]
        acc[s, c] += vals_ref[b].astype(jnp.float32)
        return carry

    lax.fori_loop(0, live, add, 0)

    @pl.when(turn == pl.num_programs(0) - 1)
    def _():
        def put(s, carry):
            for c in range(sources):
                for e in range(width):
                    out_ref[e, s, :, c * size:(c + 1) * size] = acc[
                        s, c, e * part:(e + 1) * part, :
                    ].astype(out_ref.dtype)
            return carry

        lax.fori_loop(0, groups, put, 0)


def dense_adjacency(vals, slots, cols, count, groups, sources, width):
    total, size, _ = vals.shape
    part = size // width
    return pl.pallas_call(
        dense_kernel,
        out_shape=jax.ShapeDtypeStruct((width, groups, part, sources * size), jnp.bfloat16),
        grid_spec=pltpu.PrefetchScalarGridSpec(
            num_scalar_prefetch=3,
            grid=(total // CHUNK,),
            in_specs=[pl.BlockSpec((CHUNK, size, size), lambda t, *_: (t, 0, 0))],
            out_specs=pl.BlockSpec(
                (width, groups, part, sources * size), lambda t, *_: (0, 0, 0, 0)
            ),
            scratch_shapes=[pltpu.VMEM((groups, sources, size, size), jnp.float32)],
        ),
        compiler_params=pltpu.CompilerParams(
            dimension_semantics=("arbitrary",), vmem_limit_bytes=56 * 1024 * 1024
        ),
    )(slots, cols, count, vals)


def layers_kernel(dense, source, embed_share, cot_share, outgoing, slots, hits,
                  final, grad,
                  asked0, asked1, layers, source2, got_f1, send_b1,
                  sum_f1, land_f1, sum_b1, land_b1, sum_f2, land_f2, sum_b2, land_b2, got_f2,
                  node_sems, line_sems):
    nodes, width = lax.axis_size("node"), lax.axis_size("edge")
    me, z = lax.axis_index("node"), lax.axis_index("edge")
    groups, part, depth = outgoing.shape
    sources = embed_share.shape[0]
    size = part * width
    f32, bf16 = jnp.float32, jnp.bfloat16

    barrier = pltpu.get_barrier_semaphore()

    def greet(k, carry):
        pl.semaphore_signal(barrier, inc=1, device_id={"node": lax.rem(me + k, nodes)},
                            device_id_type=pl.DeviceIdType.MESH)
        return carry

    lax.fori_loop(1, nodes, greet, 0)

    @pl.when(z > 0)
    def _():
        pl.semaphore_signal(barrier, inc=1, device_id={"edge": z - 1},
                            device_id_type=pl.DeviceIdType.MESH)

    @pl.when(z < width - 1)
    def _():
        pl.semaphore_signal(barrier, inc=1, device_id={"edge": z + 1},
                            device_id_type=pl.DeviceIdType.MESH)

    above = jnp.where(z < width - 1, 1, 0)
    below = jnp.where(z > 0, 1, 0)
    pl.semaphore_wait(barrier, nodes - 1 + above + below)

    class Exchange:
        def __init__(self, at, out, into):
            self.at, self.out, self.into = at, out, into

        def copy(self, k, src, dst, peer):
            return pltpu.make_async_remote_copy(
                src_ref=src, dst_ref=dst,
                send_sem=node_sems.at[self.at, 0, k], recv_sem=node_sems.at[self.at, 1, k],
                device_id={"node": peer}, device_id_type=pl.DeviceIdType.MESH)

        def start(self):
            def go(k, carry):
                peer = lax.rem(me + k, nodes)
                self.copy(k, self.out(peer), self.into(me), peer).start()
                return carry

            lax.fori_loop(1, nodes, go, 0)
            self.into(me)[...] = self.out(me)[...]

        def wait(self):
            def go(k, carry):
                peer = lax.rem(me + nodes - k, nodes)
                self.copy(k, self.into(peer), self.into(peer), peer).wait_recv()
                return carry

            lax.fori_loop(1, nodes, go, 0)

        def end(self):
            def go(k, carry):
                peer = lax.rem(me + k, nodes)
                self.copy(k, self.out(peer), self.into(me), peer).wait_send()
                return carry

            lax.fori_loop(1, nodes, go, 0)

    def line_copy(at, way, t, src, dst):
        return pltpu.make_async_remote_copy(
            src_ref=src, dst_ref=dst,
            send_sem=line_sems.at[at, 0, way, t], recv_sem=line_sems.at[at, 1, way, t],
            device_id={"edge": z + 1 if way == 0 else z - 1},
            device_id_type=pl.DeviceIdType.MESH)

    class Gather:
        def __init__(self, at, buf):
            self.at, self.buf = at, buf

        def send(self, way, t):
            chunk = self.buf.at[z - t if way == 0 else z + t]
            return line_copy(self.at, way, t, chunk, chunk)

        def sends(self, way, t):
            return ((z - t >= 0) & (z < width - 1)) if way == 0 else ((z + t < width) & (z > 0))

        def start(self):
            for way in range(2):
                @pl.when(self.sends(way, 0))
                def _(way=way):
                    self.send(way, 0).start()

        def step(self, t):
            for way in range(2):
                there = z - 1 - t if way == 0 else z + 1 + t

                @pl.when((there >= 0) if way == 0 else (there < width))
                def _(way=way, there=there):
                    chunk = self.buf.at[there]
                    line_copy(self.at, way, t, chunk, chunk).wait_recv()

                if t + 1 < width - 1:
                    @pl.when(self.sends(way, t + 1))
                    def _(way=way):
                        self.send(way, t + 1).start()

        def end(self):
            for t in range(width - 1):
                for way in range(2):
                    @pl.when(self.sends(way, t))
                    def _(way=way, t=t):
                        self.send(way, t).wait_send()

    class Reduce:
        def __init__(self, at, sums, land):
            self.at, self.sums, self.land = at, sums, land

        def chunk(self, way, t):
            return width - 1 - t if way == 0 else t

        def send(self, way, t):
            return line_copy(self.at, way, t, self.sums.at[self.chunk(way, t)],
                             self.land.at[way, t])

        def sends(self, way, t):
            d = self.chunk(way, t)
            return z < d if way == 0 else z > d

        def start(self):
            for way, first in ((0, 0), (1, width - 1)):
                @pl.when(z == first)
                def _(way=way):
                    for t in range(width - 1):
                        self.send(way, t).start()

        def step(self, t):
            for way in range(2):
                d = self.chunk(way, t)

                @pl.when(((z > 0) & (d >= z)) if way == 0 else ((z < width - 1) & (d <= z)))
                def _(way=way, d=d):
                    line_copy(self.at, way, t, self.sums.at[d], self.land.at[way, t]).wait_recv()
                    total = self.sums[d].astype(f32) + self.land[way, t].astype(f32)
                    self.sums[d] = total.astype(self.sums.dtype)

                @pl.when(((z > 0) & (z < d)) if way == 0 else ((z < width - 1) & (z > d)))
                def _(way=way):
                    self.send(way, t).start()

        def end(self):
            for t in range(width - 1):
                for way in range(2):
                    @pl.when(self.sends(way, t))
                    def _(way=way, t=t):
                        self.send(way, t).wait_send()

    def forward(x_ref, sums):
        x = x_ref[...]
        for e in range(width):
            out = jnp.dot(dense[e].reshape(groups * part, sources * size), x,
                          preferred_element_type=f32)
            sums[e] = out.reshape(groups, part, depth).astype(sums.dtype)

    def backward(asked, sums):
        y = asked[...].reshape(width * groups * part, depth)
        step = 2 * size
        for c in range(0, sources * size, step):
            a = dense[:, :, :, c:c + step].reshape(width * groups * part, step)
            out = lax.dot_general(a, y, (((0,), (0,)), ((), ())), preferred_element_type=f32)
            for g in range(2):
                for e in range(width):
                    begin = g * size + e * part
                    sums[e, c // size + g] = out[begin:begin + part].astype(sums.dtype)

    def placed(got, r):
        total = jnp.zeros((part, depth), f32)
        for i in range(groups):
            total = total + hits[r, i] * got[i].astype(f32)
        return total

    steps = range(width - 1)
    third = float(LAYERS + 1)

    ask0 = Exchange(0, lambda g: outgoing.at[g], lambda g: asked0.at[z, g])
    swap_f1 = Exchange(1, lambda g: sum_f1.at[z, g], lambda g: got_f1.at[g])
    ask1 = Exchange(2, lambda g: send_b1.at[g], lambda g: asked1.at[z, g])
    swap_f2 = Exchange(3, lambda g: sum_f2.at[z, g], lambda g: got_f2.at[g])
    red_f1, all_0 = Reduce(0, sum_f1, land_f1), Gather(1, asked0)
    red_b1, all_f = Reduce(2, sum_b1, land_b1), Gather(3, layers)
    red_f2, all_b = Reduce(4, sum_f2, land_f2), Gather(5, asked1)
    red_b2 = Reduce(6, sum_b2, land_b2)

    ask0.start()
    forward(source, sum_f1)
    red_f1.start()
    ask0.wait()
    all_0.start()
    for t in steps:
        red_f1.step(t)
        all_0.step(t)
    swap_f1.start()

    backward(asked0, sum_b1)
    red_b1.start()
    swap_f1.wait()

    def put_layer(r, carry):
        layers[z, r] = placed(got_f1, r).astype(bf16)
        return carry

    lax.fori_loop(0, sources, put_layer, 0)
    all_f.start()
    for t in steps:
        red_b1.step(t)
        all_f.step(t)

    for i in range(groups):
        send_b1[i] = sum_b1[z, slots[i]]
    ask1.start()

    for e in range(width):
        for g in range(sources):
            source2[g * size + e * part:g * size + (e + 1) * part, :] = layers[e, g]
    forward(source2, sum_f2)
    red_f2.start()
    ask1.wait()
    all_b.start()
    for t in steps:
        red_f2.step(t)
        all_b.step(t)
    swap_f2.start()

    backward(asked1, sum_b2)
    red_b2.start()
    swap_f2.wait()

    def put_final(r, carry):
        total = embed_share[r].astype(f32) + layers[z, r].astype(f32) + placed(got_f2, r)
        final[r] = (total / third).astype(bf16)
        return carry

    lax.fori_loop(0, sources, put_final, 0)
    for t in steps:
        red_b2.step(t)

    def put_grad(r, carry):
        total = cot_share[r].astype(f32) + sum_b1[z, r].astype(f32) + sum_b2[z, r]
        grad[r] = (total / third).astype(bf16)
        return carry

    lax.fori_loop(0, sources, put_grad, 0)
    for sent in (ask0, swap_f1, ask1, swap_f2, red_f1, all_0, red_b1, all_f, red_f2, all_b, red_b2):
        sent.end()


def shards(embed, cotangent, values, block_slot, block_col, block_count, slot_rows):
    width = lax.axis_size("edge")
    nodes = lax.axis_size("node")
    place = lax.axis_index("edge")
    groups = slot_rows.shape[1]
    vals = values[0, 0]
    size = vals.shape[1]
    part = size // width
    sources = embed.shape[0] // size
    depth = embed.shape[1]
    slot_index = slot_rows[0]

    dense = dense_adjacency(
        vals, block_slot[0, 0], block_col[0, 0], block_count[0], groups, sources, width
    )

    def share_of(rows):
        rows = lax.dynamic_slice_in_dim(rows, place * (sources * part), sources * part, 0)
        return rows.reshape(part, sources, depth).transpose(1, 0, 2)

    embed_share, cot_share = share_of(embed), share_of(cotangent)
    outgoing = cot_share[slot_index]
    source = embed.reshape(size, sources, depth).transpose(1, 0, 2).reshape(-1, depth)
    hits = slot_index[None, :] == jnp.arange(sources, dtype=jnp.int32)[:, None]

    f32, bf16 = jnp.float32, jnp.bfloat16
    vmem = pl.BlockSpec(memory_space=pltpu.VMEM)
    smem = pl.BlockSpec(memory_space=pltpu.SMEM)
    by_group, by_source = (groups, part, depth), (sources, part, depth)

    def sums(shape, kind):
        return [pltpu.VMEM((width,) + shape, kind), pltpu.VMEM((2, width - 1) + shape, kind)]

    final, grad = pl.pallas_call(
        layers_kernel,
        out_shape=[jax.ShapeDtypeStruct(by_source, bf16)] * 2,
        in_specs=[vmem] * 5 + [smem] * 2,
        out_specs=[vmem] * 2,
        scratch_shapes=[
            pltpu.VMEM((width,) + by_group, bf16),
            pltpu.VMEM((width,) + by_group, bf16),
            pltpu.VMEM((width,) + by_source, bf16),
            pltpu.VMEM((sources * size, depth), bf16),
            pltpu.VMEM(by_group, bf16),
            pltpu.VMEM(by_group, bf16),
        ]
        + sums(by_group, bf16) + sums(by_source, bf16)
        + sums(by_group, f32) + sums(by_source, f32)
        + [
            pltpu.VMEM(by_group, f32),
            pltpu.SemaphoreType.DMA((4, 2, nodes)),
            pltpu.SemaphoreType.DMA((7, 2, 2, width - 1)),
        ],
        compiler_params=pltpu.CompilerParams(
            collective_id=0, has_side_effects=True, vmem_limit_bytes=56 * 1024 * 1024
        ),
    )(dense, source, embed_share, cot_share, outgoing, slot_index, hits.astype(f32))

    def in_order(blocks):
        return blocks.transpose(1, 0, 2).reshape(part * sources, depth)

    return in_order(final), in_order(grad)


def solution(mesh):
    placed = (
        P("node", None),
        P("node", None),
        P("node", "edge", None, None, None),
        P("node", "edge", None),
        P("node", "edge", None),
        P("node", "edge"),
        P("node", None),
    )
    return jax.shard_map(
        shards,
        mesh=mesh,
        in_specs=placed,
        out_specs=(P(("node", "edge"), None), P(("node", "edge"), None)),
        check_vma=False,
    )
```

```python
import jax
import jax.numpy as jnp
from jax import lax
from jax.experimental import pallas as pl
from jax.experimental.pallas import tpu as pltpu
from jax.sharding import PartitionSpec as P

LAYERS = 2
CHUNK = 16


def dense_kernel(slots_ref, cols_ref, count_ref, vals_ref, out_ref, acc):
    turn = pl.program_id(0)
    groups, sources, size, _ = acc.shape
    width, _, part, _ = out_ref.shape

    @pl.when(turn == 0)
    def _():
        acc[...] = jnp.zeros_like(acc)

    begin = turn * CHUNK
    live = jnp.clip(count_ref[0] - begin, 0, CHUNK)

    def add(b, carry):
        s, c = slots_ref[begin + b], cols_ref[begin + b]
        acc[s, c] += vals_ref[b].astype(jnp.float32)
        return carry

    lax.fori_loop(0, live, add, 0)

    @pl.when(turn == pl.num_programs(0) - 1)
    def _():
        def put(s, carry):
            for c in range(sources):
                for e in range(width):
                    out_ref[e, s, :, c * size:(c + 1) * size] = acc[
                        s, c, e * part:(e + 1) * part, :
                    ].astype(out_ref.dtype)
            return carry

        lax.fori_loop(0, groups, put, 0)


def dense_adjacency(vals, slots, cols, count, groups, sources, width):
    total, size, _ = vals.shape
    part = size // width
    return pl.pallas_call(
        dense_kernel,
        out_shape=jax.ShapeDtypeStruct((width, groups, part, sources * size), jnp.bfloat16),
        grid_spec=pltpu.PrefetchScalarGridSpec(
            num_scalar_prefetch=3,
            grid=(total // CHUNK,),
            in_specs=[pl.BlockSpec((CHUNK, size, size), lambda t, *_: (t, 0, 0))],
            out_specs=pl.BlockSpec(
                (width, groups, part, sources * size), lambda t, *_: (0, 0, 0, 0)
            ),
            scratch_shapes=[pltpu.VMEM((groups, sources, size, size), jnp.float32)],
        ),
        compiler_params=pltpu.CompilerParams(
            dimension_semantics=("arbitrary",), vmem_limit_bytes=56 * 1024 * 1024
        ),
    )(slots, cols, count, vals)


def layers_kernel(dense, source, embed_share, cot_share, outgoing, slots, hits,
                  final, grad,
                  asked0, asked1, layers, source2, got_f1, send_b1,
                  sum_f1, land_f1, sum_b1, land_b1, sum_f2, send_f2, land_f2, sum_b2, land_b2, got_f2,
                  node_sems, line_sems):
    nodes, width = lax.axis_size("node"), lax.axis_size("edge")
    me, z = lax.axis_index("node"), lax.axis_index("edge")
    groups, _, part, depth = outgoing.shape
    sources = embed_share.shape[0]
    size = part * width
    f32, bf16 = jnp.float32, jnp.bfloat16

    barrier = pltpu.get_barrier_semaphore()

    def greet(k, carry):
        pl.semaphore_signal(barrier, inc=1, device_id={"node": lax.rem(me + k, nodes)},
                            device_id_type=pl.DeviceIdType.MESH)
        return carry

    lax.fori_loop(1, nodes, greet, 0)

    def greet_edge(k, carry):
        pl.semaphore_signal(barrier, inc=1, device_id={"edge": lax.rem(z + k, width)},
                            device_id_type=pl.DeviceIdType.MESH)
        return carry

    lax.fori_loop(1, width, greet_edge, 0)
    pl.semaphore_wait(barrier, nodes + width - 2)

    class Exchange:
        def __init__(self, at, out, into):
            self.at, self.out, self.into = at, out, into

        def copy(self, k, src, dst, peer):
            return pltpu.make_async_remote_copy(
                src_ref=src, dst_ref=dst,
                send_sem=node_sems.at[self.at, 0, k], recv_sem=node_sems.at[self.at, 1, k],
                device_id={"node": peer}, device_id_type=pl.DeviceIdType.MESH)

        def start(self):
            def go(k, carry):
                peer = lax.rem(me + k, nodes)
                self.copy(k, self.out(peer), self.into(me), peer).start()
                return carry

            lax.fori_loop(1, nodes, go, 0)
            self.into(me)[...] = self.out(me)[...]

        def wait(self):
            def go(k, carry):
                peer = lax.rem(me + nodes - k, nodes)
                self.copy(k, self.into(peer), self.into(peer), peer).wait_recv()
                return carry

            lax.fori_loop(1, nodes, go, 0)

        def end(self):
            def go(k, carry):
                peer = lax.rem(me + k, nodes)
                self.copy(k, self.out(peer), self.into(me), peer).wait_send()
                return carry

            lax.fori_loop(1, nodes, go, 0)

    def edge_copy(at, k, src, dst, peer):
        return pltpu.make_async_remote_copy(
            src_ref=src, dst_ref=dst,
            send_sem=line_sems.at[at, 0, k - 1], recv_sem=line_sems.at[at, 1, k - 1],
            device_id={"edge": peer}, device_id_type=pl.DeviceIdType.MESH)

    def after(k):
        return lax.rem(z + k, width)

    def before(k):
        return lax.rem(z + width - k, width)

    class Gather:
        def __init__(self, at, buf):
            self.at, self.buf = at, buf

        def send(self, k):
            return edge_copy(self.at, k, self.buf.at[z], self.buf.at[z], after(k))

        def start(self):
            for k in range(1, width):
                self.send(k).start()

        def step(self, t):
            chunk = self.buf.at[before(t + 1)]
            edge_copy(self.at, t + 1, chunk, chunk, before(t + 1)).wait_recv()

        def end(self):
            for k in range(1, width):
                self.send(k).wait_send()

    class Reduce:
        def __init__(self, at, sums, land, out=None):
            self.at, self.sums, self.land = at, sums, land
            self.out = sums if out is None else out

        def send(self, k):
            return edge_copy(self.at, k, self.out.at[after(k)], self.land.at[k - 1], after(k))

        def start(self):
            for k in range(1, width):
                self.send(k).start()

        def step(self, t):
            edge_copy(self.at, t + 1, self.land.at[t], self.land.at[t], before(t + 1)).wait_recv()
            if t == width - 2:
                total = self.sums[z].astype(f32)
                for k in range(width - 1):
                    total = total + self.land[k].astype(f32)
                self.sums[z] = total.astype(self.sums.dtype)

        def end(self):
            for k in range(1, width):
                self.send(k).wait_send()

    def forward(x_ref, sums, wide=None):
        x = x_ref[...]
        for e in range(width):
            out = jnp.dot(dense[e].reshape(groups * part, sources * size), x,
                          preferred_element_type=f32)
            out = out.reshape(groups, part, depth)
            sums[e] = out.astype(sums.dtype)
            if wide is not None:
                wide[e] = out

    def backward(asked, sums):
        y = asked[...].reshape(width * groups * part, depth)
        step = 2 * size
        for c in range(0, sources * size, step):
            a = dense[:, :, :, c:c + step].reshape(width * groups * part, step)
            out = lax.dot_general(a, y, (((0,), (0,)), ((), ())), preferred_element_type=f32)
            for g in range(2):
                for e in range(width):
                    begin = g * size + e * part
                    sums[e, c // size + g] = out[begin:begin + part].astype(sums.dtype)

    def placed(got, r):
        total = jnp.zeros((part, depth), f32)
        for i in range(groups):
            total = total + hits[r, i] * got[i].astype(f32)
        return total

    steps = range(width - 1)
    third = float(LAYERS + 1)

    ask0 = Exchange(0, lambda g: outgoing.at[g], lambda g: asked0.at[:, g])
    swap_f1 = Exchange(1, lambda g: sum_f1.at[z, g], lambda g: got_f1.at[g])
    ask1 = Exchange(2, lambda g: send_b1.at[g], lambda g: asked1.at[z, g])
    swap_f2 = Exchange(3, lambda g: sum_f2.at[z, g], lambda g: got_f2.at[g])
    red_f1 = Reduce(0, sum_f1, land_f1)
    red_b1, all_f = Reduce(1, sum_b1, land_b1), Gather(2, layers)
    red_f2, all_b = Reduce(3, sum_f2, land_f2, send_f2), Gather(4, asked1)
    red_b2 = Reduce(5, sum_b2, land_b2)

    def arrive(moved):
        for t in steps:
            moved.step(t)

    ask0.start()
    forward(source, sum_f1)
    red_f1.start()
    ask0.wait()
    backward(asked0, sum_b1)
    red_b1.start()
    arrive(red_f1)
    swap_f1.start()
    swap_f1.wait()

    def put_layer(r, carry):
        layers[z, r] = placed(got_f1, r).astype(bf16)
        return carry

    lax.fori_loop(0, sources, put_layer, 0)
    all_f.start()
    arrive(red_b1)
    for i in range(groups):
        send_b1[i] = sum_b1[z, slots[i]]
    ask1.start()
    ask1.wait()
    all_b.start()
    arrive(all_f)
    for e in range(width):
        for g in range(sources):
            source2[g * size + e * part:g * size + (e + 1) * part, :] = layers[e, g]
    forward(source2, send_f2, sum_f2)
    red_f2.start()
    arrive(all_b)
    backward(asked1, sum_b2)
    red_b2.start()
    arrive(red_f2)
    swap_f2.start()
    swap_f2.wait()

    def put_final(r, carry):
        total = embed_share[r].astype(f32) + layers[z, r].astype(f32) + placed(got_f2, r)
        final[r] = (total / third).astype(bf16)
        return carry

    lax.fori_loop(0, sources, put_final, 0)
    arrive(red_b2)

    def put_grad(r, carry):
        total = cot_share[r].astype(f32) + sum_b1[z, r].astype(f32) + sum_b2[z, r]
        grad[r] = (total / third).astype(bf16)
        return carry

    lax.fori_loop(0, sources, put_grad, 0)
    for sent in (ask0, swap_f1, ask1, swap_f2, red_f1, red_b1, all_f, red_f2, all_b, red_b2):
        sent.end()


def shards(embed, cotangent, values, block_slot, block_col, block_count, slot_rows):
    width = lax.axis_size("edge")
    nodes = lax.axis_size("node")
    place = lax.axis_index("edge")
    groups = slot_rows.shape[1]
    vals = values[0, 0]
    size = vals.shape[1]
    part = size // width
    sources = embed.shape[0] // size
    depth = embed.shape[1]
    slot_index = slot_rows[0]

    dense = dense_adjacency(
        vals, block_slot[0, 0], block_col[0, 0], block_count[0], groups, sources, width
    )

    def share_of(rows):
        rows = lax.dynamic_slice_in_dim(rows, place * (sources * part), sources * part, 0)
        return rows.reshape(part, sources, depth).transpose(1, 0, 2)

    embed_share, cot_share = share_of(embed), share_of(cotangent)
    blocks = cotangent.reshape(size, sources, depth).transpose(1, 0, 2)
    outgoing = blocks[slot_index].reshape(groups, width, part, depth)
    source = embed.reshape(size, sources, depth).transpose(1, 0, 2).reshape(-1, depth)
    hits = slot_index[None, :] == jnp.arange(sources, dtype=jnp.int32)[:, None]

    f32, bf16 = jnp.float32, jnp.bfloat16
    vmem = pl.BlockSpec(memory_space=pltpu.VMEM)
    smem = pl.BlockSpec(memory_space=pltpu.SMEM)
    by_group, by_source = (groups, part, depth), (sources, part, depth)

    def sums(shape, kind):
        return [pltpu.VMEM((width,) + shape, kind), pltpu.VMEM((width - 1,) + shape, kind)]

    final, grad = pl.pallas_call(
        layers_kernel,
        out_shape=[jax.ShapeDtypeStruct(by_source, bf16)] * 2,
        in_specs=[vmem] * 5 + [smem] * 2,
        out_specs=[vmem] * 2,
        scratch_shapes=[
            pltpu.VMEM((width,) + by_group, bf16),
            pltpu.VMEM((width,) + by_group, bf16),
            pltpu.VMEM((width,) + by_source, bf16),
            pltpu.VMEM((sources * size, depth), bf16),
            pltpu.VMEM(by_group, bf16),
            pltpu.VMEM(by_group, bf16),
        ]
        + sums(by_group, bf16) + sums(by_source, bf16)
        + [pltpu.VMEM((width,) + by_group, f32)]
        + sums(by_group, bf16) + sums(by_source, f32)
        + [
            pltpu.VMEM(by_group, f32),
            pltpu.SemaphoreType.DMA((4, 2, nodes)),
            pltpu.SemaphoreType.DMA((6, 2, width - 1)),
        ],
        compiler_params=pltpu.CompilerParams(
            collective_id=0, has_side_effects=True, vmem_limit_bytes=56 * 1024 * 1024
        ),
    )(dense, source, embed_share, cot_share, outgoing, slot_index, hits.astype(f32))

    def in_order(blocks):
        return blocks.transpose(1, 0, 2).reshape(part * sources, depth)

    return in_order(final), in_order(grad)


def solution(mesh):
    placed = (
        P("node", None),
        P("node", None),
        P("node", "edge", None, None, None),
        P("node", "edge", None),
        P("node", "edge", None),
        P("node", "edge"),
        P("node", None),
    )
    return jax.shard_map(
        shards,
        mesh=mesh,
        in_specs=placed,
        out_specs=(P(("node", "edge"), None), P(("node", "edge"), None)),
        check_vma=False,
    )
```

```python
import jax
import jax.numpy as jnp
from jax import lax
from jax.experimental import pallas as pl
from jax.experimental.pallas import tpu as pltpu
from jax.sharding import PartitionSpec as P

LAYERS = 2
CHUNK = 16


def dense_kernel(slots_ref, cols_ref, count_ref, vals_ref, out_ref, acc):
    turn = pl.program_id(0)
    groups, sources, size, _ = acc.shape
    width, _, part, _ = out_ref.shape

    @pl.when(turn == 0)
    def _():
        acc[...] = jnp.zeros_like(acc)

    begin = turn * CHUNK
    live = jnp.clip(count_ref[0] - begin, 0, CHUNK)

    def add(b, carry):
        s, c = slots_ref[begin + b], cols_ref[begin + b]
        acc[s, c] += vals_ref[b].astype(jnp.float32)
        return carry

    lax.fori_loop(0, live, add, 0)

    @pl.when(turn == pl.num_programs(0) - 1)
    def _():
        def put(s, carry):
            for c in range(sources):
                for e in range(width):
                    out_ref[e, s, :, c * size:(c + 1) * size] = acc[
                        s, c, e * part:(e + 1) * part, :
                    ].astype(out_ref.dtype)
            return carry

        lax.fori_loop(0, groups, put, 0)


def dense_adjacency(vals, slots, cols, count, groups, sources, width):
    total, size, _ = vals.shape
    part = size // width
    return pl.pallas_call(
        dense_kernel,
        out_shape=jax.ShapeDtypeStruct((width, groups, part, sources * size), jnp.bfloat16),
        grid_spec=pltpu.PrefetchScalarGridSpec(
            num_scalar_prefetch=3,
            grid=(total // CHUNK,),
            in_specs=[pl.BlockSpec((CHUNK, size, size), lambda t, *_: (t, 0, 0))],
            out_specs=pl.BlockSpec(
                (width, groups, part, sources * size), lambda t, *_: (0, 0, 0, 0)
            ),
            scratch_shapes=[pltpu.VMEM((groups, sources, size, size), jnp.float32)],
        ),
        compiler_params=pltpu.CompilerParams(
            dimension_semantics=("arbitrary",), vmem_limit_bytes=56 * 1024 * 1024
        ),
    )(slots, cols, count, vals)


def layers_kernel(dense, source, embed_share, cot_share, outgoing, slots, hits,
                  final, grad,
                  asked0, asked1, layers, source2, got_f1, send_b1,
                  sum_f1, land_f1, sum_b1, land_b1, sum_f2, send_f2, land_f2, sum_b2, send_b2, land_b2,
                  mean_f2, land_mf2, mean_b2, land_mb2, got_f2,
                  node_sems, line_sems):
    nodes, width = lax.axis_size("node"), lax.axis_size("edge")
    me, z = lax.axis_index("node"), lax.axis_index("edge")
    groups, _, part, depth = outgoing.shape
    sources = embed_share.shape[0]
    size = part * width
    f32, bf16 = jnp.float32, jnp.bfloat16

    barrier = pltpu.get_barrier_semaphore()

    def greet(k, carry):
        pl.semaphore_signal(barrier, inc=1, device_id={"node": lax.rem(me + k, nodes)},
                            device_id_type=pl.DeviceIdType.MESH)
        return carry

    lax.fori_loop(1, nodes, greet, 0)

    def greet_edge(k, carry):
        pl.semaphore_signal(barrier, inc=1, device_id={"edge": lax.rem(z + k, width)},
                            device_id_type=pl.DeviceIdType.MESH)
        return carry

    lax.fori_loop(1, width, greet_edge, 0)
    pl.semaphore_wait(barrier, nodes + width - 2)

    class Exchange:
        def __init__(self, at, out, into):
            self.at, self.out, self.into = at, out, into

        def copy(self, k, src, dst, peer):
            return pltpu.make_async_remote_copy(
                src_ref=src, dst_ref=dst,
                send_sem=node_sems.at[self.at, 0, k], recv_sem=node_sems.at[self.at, 1, k],
                device_id={"node": peer}, device_id_type=pl.DeviceIdType.MESH)

        def start(self):
            def go(k, carry):
                peer = lax.rem(me + k, nodes)
                self.copy(k, self.out(peer), self.into(me), peer).start()
                return carry

            lax.fori_loop(1, nodes, go, 0)
            self.into(me)[...] = self.out(me)[...]

        def wait(self):
            def go(k, carry):
                peer = lax.rem(me + nodes - k, nodes)
                self.copy(k, self.into(peer), self.into(peer), peer).wait_recv()
                return carry

            lax.fori_loop(1, nodes, go, 0)

        def end(self):
            def go(k, carry):
                peer = lax.rem(me + k, nodes)
                self.copy(k, self.out(peer), self.into(me), peer).wait_send()
                return carry

            lax.fori_loop(1, nodes, go, 0)

    def edge_copy(at, k, src, dst, peer):
        return pltpu.make_async_remote_copy(
            src_ref=src, dst_ref=dst,
            send_sem=line_sems.at[at, 0, k - 1], recv_sem=line_sems.at[at, 1, k - 1],
            device_id={"edge": peer}, device_id_type=pl.DeviceIdType.MESH)

    def after(k):
        return lax.rem(z + k, width)

    def before(k):
        return lax.rem(z + width - k, width)

    class Gather:
        def __init__(self, at, buf):
            self.at, self.buf = at, buf

        def send(self, k):
            return edge_copy(self.at, k, self.buf.at[z], self.buf.at[z], after(k))

        def start(self):
            for k in range(1, width):
                self.send(k).start()

        def step(self, t):
            chunk = self.buf.at[before(t + 1)]
            edge_copy(self.at, t + 1, chunk, chunk, before(t + 1)).wait_recv()

        def end(self):
            for k in range(1, width):
                self.send(k).wait_send()

    class Reduce:
        def __init__(self, at, sums, land, out=None):
            self.at, self.sums, self.land = at, sums, land
            self.out = sums if out is None else out

        def send(self, k):
            return edge_copy(self.at, k, self.out.at[after(k)], self.land.at[k - 1], after(k))

        def start(self):
            for k in range(1, width):
                self.send(k).start()

        def step(self, t):
            edge_copy(self.at, t + 1, self.land.at[t], self.land.at[t], before(t + 1)).wait_recv()
            if t == width - 2:
                total = self.sums[z].astype(f32)
                for k in range(width - 1):
                    total = total + self.land[k].astype(f32)
                self.sums[z] = total.astype(self.sums.dtype)

        def end(self):
            for k in range(1, width):
                self.send(k).wait_send()

    def forward(x_ref, sums, wide=None, means=None):
        x = x_ref[...]
        for e in range(width):
            out = jnp.dot(dense[e].reshape(groups * part, sources * size), x,
                          preferred_element_type=f32)
            out = out.reshape(groups, part, depth)
            if wide is not None:
                middle = jnp.mean(out, axis=1)
                means[e] = middle
                out = out - middle[:, None, :]
                wide[e] = out
            sums[e] = out.astype(sums.dtype)

    def backward(asked, sums, wide=None, means=None):
        y = asked[...].reshape(width * groups * part, depth)
        step = 2 * size
        for c in range(0, sources * size, step):
            a = dense[:, :, :, c:c + step].reshape(width * groups * part, step)
            out = lax.dot_general(a, y, (((0,), (0,)), ((), ())), preferred_element_type=f32)
            for g in range(2):
                for e in range(width):
                    begin = g * size + e * part
                    block = out[begin:begin + part]
                    if wide is not None:
                        middle = jnp.mean(block, axis=0, keepdims=True)
                        means[e, c // size + g:c // size + g + 1, :] = middle
                        block = block - middle
                        wide[e, c // size + g] = block
                    sums[e, c // size + g] = block.astype(sums.dtype)

    def placed(got, r):
        total = jnp.zeros((part, depth), f32)
        for i in range(groups):
            total = total + hits[r, i] * got[i].astype(f32)
        return total

    steps = range(width - 1)
    third = float(LAYERS + 1)

    ask0 = Exchange(0, lambda g: outgoing.at[g], lambda g: asked0.at[:, g])
    swap_f1 = Exchange(1, lambda g: sum_f1.at[z, g], lambda g: got_f1.at[g])
    ask1 = Exchange(2, lambda g: send_b1.at[g], lambda g: asked1.at[z, g])
    swap_f2 = Exchange(3, lambda g: sum_f2.at[z, g], lambda g: got_f2.at[g])
    red_f1 = Reduce(0, sum_f1, land_f1)
    red_b1, all_f = Reduce(1, sum_b1, land_b1), Gather(2, layers)
    red_f2, all_b = Reduce(3, sum_f2, land_f2, send_f2), Gather(4, asked1)
    red_b2 = Reduce(5, sum_b2, land_b2, send_b2)
    mid_f2, mid_b2 = Reduce(6, mean_f2, land_mf2), Reduce(7, mean_b2, land_mb2)

    def arrive(moved):
        for t in steps:
            moved.step(t)

    ask0.start()
    forward(source, sum_f1)
    red_f1.start()
    ask0.wait()
    backward(asked0, sum_b1)
    red_b1.start()
    arrive(red_f1)
    swap_f1.start()
    swap_f1.wait()

    def put_layer(r, carry):
        layers[z, r] = placed(got_f1, r).astype(bf16)
        return carry

    lax.fori_loop(0, sources, put_layer, 0)
    all_f.start()
    arrive(red_b1)
    for i in range(groups):
        send_b1[i] = sum_b1[z, slots[i]]
    ask1.start()
    ask1.wait()
    all_b.start()
    arrive(all_f)
    for e in range(width):
        for g in range(sources):
            source2[g * size + e * part:g * size + (e + 1) * part, :] = layers[e, g]
    forward(source2, send_f2, sum_f2, mean_f2)
    mid_f2.start()
    red_f2.start()
    arrive(all_b)
    backward(asked1, send_b2, sum_b2, mean_b2)
    mid_b2.start()
    red_b2.start()
    arrive(mid_f2)
    arrive(red_f2)
    sum_f2[z] = sum_f2[z] + mean_f2[z][:, None, :]
    swap_f2.start()
    swap_f2.wait()

    def put_final(r, carry):
        total = embed_share[r].astype(f32) + layers[z, r].astype(f32) + placed(got_f2, r)
        final[r] = (total / third).astype(bf16)
        return carry

    lax.fori_loop(0, sources, put_final, 0)
    arrive(mid_b2)
    arrive(red_b2)
    sum_b2[z] = sum_b2[z] + mean_b2[z][:, None, :]

    def put_grad(r, carry):
        total = cot_share[r].astype(f32) + sum_b1[z, r].astype(f32) + sum_b2[z, r]
        grad[r] = (total / third).astype(bf16)
        return carry

    lax.fori_loop(0, sources, put_grad, 0)
    for sent in (ask0, swap_f1, ask1, swap_f2, red_f1, red_b1, all_f, red_f2, all_b, red_b2, mid_f2, mid_b2):
        sent.end()


def shards(embed, cotangent, values, block_slot, block_col, block_count, slot_rows):
    width = lax.axis_size("edge")
    nodes = lax.axis_size("node")
    place = lax.axis_index("edge")
    groups = slot_rows.shape[1]
    vals = values[0, 0]
    size = vals.shape[1]
    part = size // width
    sources = embed.shape[0] // size
    depth = embed.shape[1]
    slot_index = slot_rows[0]

    dense = dense_adjacency(
        vals, block_slot[0, 0], block_col[0, 0], block_count[0], groups, sources, width
    )

    def share_of(rows):
        rows = lax.dynamic_slice_in_dim(rows, place * (sources * part), sources * part, 0)
        return rows.reshape(part, sources, depth).transpose(1, 0, 2)

    embed_share, cot_share = share_of(embed), share_of(cotangent)
    blocks = cotangent.reshape(size, sources, depth).transpose(1, 0, 2)
    outgoing = blocks[slot_index].reshape(groups, width, part, depth)
    source = embed.reshape(size, sources, depth).transpose(1, 0, 2).reshape(-1, depth)
    hits = slot_index[None, :] == jnp.arange(sources, dtype=jnp.int32)[:, None]

    f32, bf16 = jnp.float32, jnp.bfloat16
    vmem = pl.BlockSpec(memory_space=pltpu.VMEM)
    smem = pl.BlockSpec(memory_space=pltpu.SMEM)
    by_group, by_source = (groups, part, depth), (sources, part, depth)

    def sums(shape, kind):
        return [pltpu.VMEM((width,) + shape, kind), pltpu.VMEM((width - 1,) + shape, kind)]

    final, grad = pl.pallas_call(
        layers_kernel,
        out_shape=[jax.ShapeDtypeStruct(by_source, bf16)] * 2,
        in_specs=[vmem] * 5 + [smem] * 2,
        out_specs=[vmem] * 2,
        scratch_shapes=[
            pltpu.VMEM((width,) + by_group, bf16),
            pltpu.VMEM((width,) + by_group, bf16),
            pltpu.VMEM((width,) + by_source, bf16),
            pltpu.VMEM((sources * size, depth), bf16),
            pltpu.VMEM(by_group, bf16),
            pltpu.VMEM(by_group, bf16),
        ]
        + sums(by_group, bf16) + sums(by_source, bf16)
        + [pltpu.VMEM((width,) + by_group, f32)]
        + sums(by_group, bf16) + [pltpu.VMEM((width,) + by_source, f32)]
        + sums(by_source, bf16)
        + sums((groups, depth), f32) + sums((sources, depth), f32)
        + [
            pltpu.VMEM(by_group, f32),
            pltpu.SemaphoreType.DMA((4, 2, nodes)),
            pltpu.SemaphoreType.DMA((8, 2, width - 1)),
        ],
        compiler_params=pltpu.CompilerParams(
            collective_id=0, has_side_effects=True, vmem_limit_bytes=56 * 1024 * 1024
        ),
    )(dense, source, embed_share, cot_share, outgoing, slot_index, hits.astype(f32))

    def in_order(blocks):
        return blocks.transpose(1, 0, 2).reshape(part * sources, depth)

    return in_order(final), in_order(grad)


def solution(mesh):
    placed = (
        P("node", None),
        P("node", None),
        P("node", "edge", None, None, None),
        P("node", "edge", None),
        P("node", "edge", None),
        P("node", "edge"),
        P("node", None),
    )
    return jax.shard_map(
        shards,
        mesh=mesh,
        in_specs=placed,
        out_specs=(P(("node", "edge"), None), P(("node", "edge"), None)),
        check_vma=False,
    )
```
